256 devices in a mesh: video: 16 (over z_lo, x, core), frame: 16 (over y, z_hi).
Axes of the slice: x: 4, y: 4, z: 8 (z_hi: 4, z_lo: 2; z = z_hi * 2 + z_lo), core: 2. Of those that a mesh axis runs over, the one named last changes fastest.
Arguments:
- frames: bfloat16 [256, 1024, 640], P(('video', 'frame')), parts along dimension 0, may hold values from -6 to 6
- ref_rows: bfloat16 [16384, 640], P(('video', 'frame')), parts along dimension 0, may hold values from -6 to 6
- w_query: bfloat16 [640, 640], replicated, may hold values from -1 to 1
- w_key: bfloat16 [640, 640], replicated, may hold values from -1 to 1
- w_value: bfloat16 [640, 640], replicated, may hold values from -0.25 to 0.25
- w_out: bfloat16 [640, 640], replicated, may hold values from -0.25 to 0.25
- w_conv: bfloat16 [3, 640, 640], replicated, may hold values from -0.125 to 0.125
- t_query: bfloat16 [640, 640], replicated, may hold values from -1 to 1
- t_key: bfloat16 [640, 640], replicated, may hold values from -1 to 1
- t_value: bfloat16 [640, 640], replicated, may hold values from -0.25 to 0.25
- t_out: bfloat16 [640, 640], replicated, may hold values from -0.25 to 0.25
Outputs:
- result: bfloat16 [256, 1024, 640], P(('video', 'frame')), parts along dimension 0
The draws below stay inside these ranges and needn't reach their ends.
There are 16 independent parts, one for each index of `video`. The reference program is written for one: setup_inputs(seed, part) draws one part's arguments, and reference() takes and returns one part's arrays. A program takes and returns all parts, laid end to end along the dimension named above; an argument that names none is the same for every part. Nothing has to cross between parts.
All inputs are finite; a program needn't handle non-finite values.
Results may differ from the reference program's by a relative error of at most 0.011.
Values may be sent and summed in bfloat16 or wider, within the bound.
No kernel may reach another device: no remote copies, remote signals or barrier semaphores. Data moves between devices by JAX's collectives and lax.ppermute only.
A program may use at most 128 MiB of HBM per device.

```python
import math
import jax
import jax.numpy as jnp
from jax import lax

C = 640
HEADS = 10
HW = 1024
FRAMES = 16


def own_part(key, tag):
    return jax.random.normal(jax.random.fold_in(key, tag), (C, C), jnp.float32)


def draw_w_query(key, part):
    value = own_part(key, 21) / math.sqrt(C)
    return jnp.clip(value, -1.0, 1.0).astype(jnp.bfloat16)


def draw_w_key(key, part):
    value = own_part(key, 22) / math.sqrt(C)
    return jnp.clip(value, -1.0, 1.0).astype(jnp.bfloat16)


def draw_t_query(key, part):
    value = own_part(key, 23) / math.sqrt(C)
    return jnp.clip(value, -1.0, 1.0).astype(jnp.bfloat16)


def draw_t_key(key, part):
    value = own_part(key, 24) / math.sqrt(C)
    return jnp.clip(value, -1.0, 1.0).astype(jnp.bfloat16)


def shard_levels(stream_key, extent, shards, least, largest):
    factor_of, own = 1.0, jax.random.fold_in(stream_key, 6)
    for axis_at, blocks in shards:
        heights = jnp.exp(jax.random.uniform(jax.random.fold_in(own, axis_at), (blocks,), jnp.float32, least / len(shards), largest / len(shards)))
        factor_of = factor_of * jnp.repeat(heights, extent[axis_at] // blocks).reshape([-1 if axis == axis_at else 1 for axis in range(len(extent))])
    return factor_of


def centred(key, shape, scale, reach, pieces=(), dtype=jnp.bfloat16):
    entries = jax.random.normal(key, shape, jnp.float32) * scale
    if len(pieces) > 0:
        entries = shard_levels(key, shape, pieces, -0.22, 0.18) * entries
    return jnp.clip(entries, min=-reach, max=reach).astype(dtype)


def setup_inputs(seed: int = 0, part: int = 0) -> dict:
    arg_keys = jax.random.split(jax.random.key(seed), 12)
    part_splits = jax.random.split(jax.random.fold_in(arg_keys[11], part), 12)
    frames = centred(part_splits[0], (FRAMES, HW, C), 1.0, 6.0, ((0, 16),))
    ref_rows = centred(part_splits[1], (HW, C), 1.0, 6.0, ((0, 16),))
    w_query = draw_w_query(jax.random.fold_in(arg_keys[11], 71), part)
    w_key = draw_w_key(jax.random.fold_in(arg_keys[11], 71), part)
    w_value = centred(arg_keys[4], (C, C), C ** -0.5, 0.25)
    w_out = centred(arg_keys[5], (C, C), C ** -0.5, 0.25)
    w_conv = centred(arg_keys[6], (3, C, C), (3 * C) ** -0.5, 0.125)
    t_query = draw_t_query(jax.random.fold_in(arg_keys[11], 71), part)
    t_key = draw_t_key(jax.random.fold_in(arg_keys[11], 71), part)
    t_value = centred(arg_keys[9], (C, C), C ** -0.5, 0.25)
    t_out = centred(arg_keys[10], (C, C), C ** -0.5, 0.25)
    return dict(frames=frames, ref_rows=ref_rows, w_query=w_query, w_key=w_key, w_value=w_value, w_out=w_out, w_conv=w_conv, t_query=t_query, t_key=t_key, t_value=t_value, t_out=t_out)


def rounded(value):
    return lax.optimization_barrier(value.astype(jnp.bfloat16)).astype(jnp.float32)

def layer_norm(value):
    mean = lax.optimization_barrier(jnp.mean(value, axis=-1, keepdims=True))
    centered = value - mean
    var = lax.optimization_barrier(jnp.mean(centered * centered, axis=-1, keepdims=True))
    return centered * lax.rsqrt(var + 1e-05)

def project(rows, weight):
    return jnp.dot(rows, weight, preferred_element_type=jnp.float32).astype(jnp.bfloat16)

def reference(frames, ref_rows, w_query, w_key, w_value, w_out, w_conv, t_query, t_key, t_value, t_out):
    nframes, pixels, width = frames.shape
    head_dim = width // HEADS
    scale = 1.0 / math.sqrt(head_dim)
    normed = layer_norm(frames.astype(jnp.float32)).astype(jnp.bfloat16).reshape(-1, width)
    query = project(normed, w_query).astype(jnp.float32).reshape(nframes, pixels, HEADS, head_dim)
    keys = project(normed, w_key).astype(jnp.float32).reshape(nframes, pixels, HEADS, head_dim)
    values = project(normed, w_value).astype(jnp.float32).reshape(nframes, pixels, HEADS, head_dim)
    ref_keys = project(ref_rows, w_key).astype(jnp.float32).reshape(pixels, HEADS, head_dim)
    ref_values = project(ref_rows, w_value).astype(jnp.float32).reshape(pixels, HEADS, head_dim)

    def one_head(args):
        qa, ka, va, rka, rva = args
        own = jnp.einsum('fqd,fkd->fqk', qa, ka) * scale
        far = jnp.einsum('fqd,kd->fqk', qa, rka) * scale
        scores = jnp.concatenate([own, far], axis=-1)
        peak = lax.optimization_barrier(jnp.max(scores, axis=-1, keepdims=True))
        expo = jnp.exp(scores - peak)
        total = lax.optimization_barrier(jnp.sum(expo, axis=-1))
        weights = rounded(expo)
        mixed = jnp.einsum('fqk,fkd->fqd', weights[:, :, :pixels], va)
        mixed = mixed + jnp.einsum('fqk,kd->fqd', weights[:, :, pixels:], rva)
        return mixed / total[..., None]
    per_head = lax.map(one_head, (query.transpose(2, 0, 1, 3), keys.transpose(2, 0, 1, 3), values.transpose(2, 0, 1, 3), ref_keys.transpose(1, 0, 2), ref_values.transpose(1, 0, 2)))
    attended = per_head.transpose(1, 2, 0, 3).reshape(-1, width).astype(jnp.bfloat16)
    first = (frames.astype(jnp.float32) + jnp.dot(attended, w_out, preferred_element_type=jnp.float32).reshape(nframes, pixels, width)).astype(jnp.bfloat16)
    padded = jnp.pad(first, ((1, 1), (0, 0), (0, 0)))
    conv = jnp.zeros((nframes * pixels, width), jnp.float32)
    for tap in range(3):
        conv = conv + jnp.dot(padded[tap:tap + nframes].reshape(-1, width), w_conv[tap], preferred_element_type=jnp.float32)
    second = (first.astype(jnp.float32) + conv.reshape(nframes, pixels, width)).astype(jnp.bfloat16)
    normed2 = layer_norm(second.astype(jnp.float32)).astype(jnp.bfloat16).reshape(-1, width)
    tquery = project(normed2, t_query).astype(jnp.float32).reshape(nframes, pixels, HEADS, head_dim)
    tkeys = project(normed2, t_key).astype(jnp.float32).reshape(nframes, pixels, HEADS, head_dim)
    tvalues = project(normed2, t_value).astype(jnp.float32).reshape(nframes, pixels, HEADS, head_dim)
    tscores = jnp.einsum('fnhd,gnhd->nhfg', tquery, tkeys) * scale
    tpeak = lax.optimization_barrier(jnp.max(tscores, axis=-1, keepdims=True))
    texpo = jnp.exp(tscores - tpeak)
    ttotal = lax.optimization_barrier(jnp.sum(texpo, axis=-1))
    tmixed = jnp.einsum('nhfg,gnhd->nhfd', rounded(texpo), tvalues) / ttotal[..., None]
    tattended = tmixed.transpose(2, 0, 1, 3).reshape(-1, width).astype(jnp.bfloat16)
    result = second.astype(jnp.float32) + jnp.dot(tattended, t_out, preferred_element_type=jnp.float32).reshape(nframes, pixels, width)
    return result.astype(jnp.bfloat16)
```

```python
import math

import jax
import jax.numpy as jnp
from jax import lax
from jax.experimental import pallas as pl
from jax.experimental.pallas import tpu as pltpu
from jax.sharding import PartitionSpec as P

HEADS = 10
LOG2E = 1.4426950408889634
BF16 = jnp.bfloat16
F32 = jnp.float32
VMEM_LIMIT = 48 * 1024 * 1024


def params():
    return pltpu.CompilerParams(vmem_limit_bytes=VMEM_LIMIT)


def norm_rows(value):
    mean = jnp.mean(value, axis=-1, keepdims=True)
    centered = value - mean
    var = jnp.mean(centered * centered, axis=-1, keepdims=True)
    return (centered * lax.rsqrt(var + 1e-05)).astype(BF16)


def mm(a, b):
    return jnp.dot(a, b, preferred_element_type=F32)


def mm_t(a, b):
    return lax.dot_general(a, b, (((1,), (1,)), ((), ())), preferred_element_type=F32)


def qkv_kernel(scale, x_ref, wq_ref, wk_ref, wv_ref, q_ref, kt_ref, v_ref):
    normed = norm_rows(x_ref[0].astype(F32))
    q_ref[...] = (mm(normed, wq_ref[...]) * scale).astype(BF16)
    kt_ref[...] = mm(normed, wk_ref[...]).astype(BF16).T
    v_ref[...] = mm(normed, wv_ref[...]).astype(BF16)


def qkv(frames, w_query, w_key, w_value, scale, block=256):
    _, pixels, width = frames.shape
    weight = pl.BlockSpec((width, width), lambda i: (0, 0))
    rows = pl.BlockSpec((block, width), lambda i: (i, 0))
    return pl.pallas_call(
        lambda *refs: qkv_kernel(scale, *refs),
        grid=(pixels // block,),
        in_specs=[pl.BlockSpec((1, block, width), lambda i: (0, i, 0)), weight, weight, weight],
        out_specs=[rows, pl.BlockSpec((width, block), lambda i: (0, i)), rows],
        out_shape=[
            jax.ShapeDtypeStruct((pixels, width), BF16),
            jax.ShapeDtypeStruct((width, pixels), BF16),
            jax.ShapeDtypeStruct((pixels, width), BF16),
        ],
        compiler_params=params(),
        cost_estimate=pl.CostEstimate(
            flops=6 * pixels * width * width,
            bytes_accessed=2 * (4 * pixels * width + 3 * width * width),
            transcendentals=0,
        ),
        name="qkv",
    )(frames, w_query, w_key, w_value)


def ref_kernel(x_ref, wk_ref, wv_ref, kt_ref, v_ref):
    rows = x_ref[...]
    kt_ref[...] = mm(rows, wk_ref[...]).astype(BF16).T
    v_ref[...] = mm(rows, wv_ref[...]).astype(BF16)


def ref_kv(rows, w_key, w_value, block=256):
    count, width = rows.shape
    weight = pl.BlockSpec((width, width), lambda i: (0, 0))
    spec = pl.BlockSpec((block, width), lambda i: (i, 0))
    return pl.pallas_call(
        ref_kernel,
        grid=(count // block,),
        in_specs=[spec, weight, weight],
        out_specs=[pl.BlockSpec((width, block), lambda i: (0, i)), spec],
        out_shape=[
            jax.ShapeDtypeStruct((width, count), BF16),
            jax.ShapeDtypeStruct((count, width), BF16),
        ],
        compiler_params=params(),
        cost_estimate=pl.CostEstimate(
            flops=4 * count * width * width,
            bytes_accessed=2 * (3 * count * width + 2 * width * width),
            transcendentals=0,
        ),
        name="ref_kv",
    )(rows, w_key, w_value)


def attend_pair(q_pair, score, values, ones, low):
    zero = jnp.zeros_like(q_pair)
    halves = []
    for half in range(2):
        q_one = jnp.where(low == (half == 0), q_pair, zero)
        scores = score(q_one)
        peak = jnp.max(scores, axis=-1, keepdims=True)
        expo = jnp.exp2(scores - peak).astype(BF16)
        mixed = mm(expo, jnp.concatenate([values, ones], axis=1))
        halves.append(mixed[:, :128] / mixed[:, 128:])
    return jnp.where(low, halves[0], halves[1]).astype(BF16)


def spatial_kernel(x_ref, q_ref, kt_ref, v_ref, rkt_ref, rv_ref, wo_ref, out_ref):
    block, width = q_ref.shape
    low = lax.broadcasted_iota(jnp.int32, (block, 128), 1) < 64
    ones = jnp.ones((kt_ref.shape[1] + rkt_ref.shape[1], 128), BF16)
    attended = []
    for pair in range(width // 128):
        lanes = slice(pair * 128, pair * 128 + 128)
        kt = jnp.concatenate([kt_ref[lanes, :], rkt_ref[lanes, :]], axis=1)
        values = jnp.concatenate([v_ref[:, lanes], rv_ref[:, lanes]], axis=0)
        attended.append(
            attend_pair(q_ref[:, lanes], lambda q_one: mm(q_one, kt), values, ones, low)
        )
    out = mm(jnp.concatenate(attended, axis=1), wo_ref[...])
    out_ref[...] = (x_ref[0].astype(F32) + out).astype(BF16)


def spatial(frames, query, kt, values, rkt, rvalues, w_out, start, count, block=256):
    _, pixels, width = frames.shape
    keys = kt.shape[1] + rkt.shape[1]
    first = start // block
    whole = lambda a: pl.BlockSpec(a.shape, lambda i: (0, 0))
    return pl.pallas_call(
        spatial_kernel,
        grid=(count // block,),
        in_specs=[
            pl.BlockSpec((1, block, width), lambda i: (0, i + first, 0)),
            pl.BlockSpec((block, width), lambda i: (i + first, 0)),
            whole(kt),
            whole(values),
            whole(rkt),
            whole(rvalues),
            whole(w_out),
        ],
        out_specs=pl.BlockSpec((block, width), lambda i: (i, 0)),
        out_shape=jax.ShapeDtypeStruct((count, width), BF16),
        compiler_params=params(),
        cost_estimate=pl.CostEstimate(
            flops=4 * count * keys * width * 3,
            bytes_accessed=2 * (3 * count * width + 2 * keys * width),
            transcendentals=count * keys * HEADS,
        ),
        name="spatial",
    )(frames, query, kt, values, rkt, rvalues, w_out)


def temporal_kernel(scale, x_ref, wc_ref, tq_ref, tk_ref, tv_ref, to_ref, out_ref):
    nframes, count, width = x_ref.shape
    rows = nframes * count
    x = x_ref[...].reshape(rows, width)
    pad = jnp.zeros((count, width), BF16)
    conv = mm(jnp.concatenate([pad, x[: rows - count]], axis=0), wc_ref[0])
    conv = conv + mm(x, wc_ref[1])
    conv = conv + mm(jnp.concatenate([x[count:], pad], axis=0), wc_ref[2])
    second = (x.astype(F32) + conv).astype(BF16).astype(F32)
    normed = norm_rows(second)
    query = (mm(normed, tq_ref[...]) * scale).astype(BF16)
    keys = mm(normed, tk_ref[...]).astype(BF16)
    values = mm(normed, tv_ref[...]).astype(BF16)
    low = lax.broadcasted_iota(jnp.int32, (rows, 128), 1) < 64
    ones = jnp.ones((rows, 128), BF16)
    mine = lax.broadcasted_iota(jnp.int32, (rows, rows), 0) % count
    theirs = lax.broadcasted_iota(jnp.int32, (rows, rows), 1) % count
    same = mine == theirs
    attended = []
    for pair in range(width // 128):
        lanes = slice(pair * 128, pair * 128 + 128)
        k_pair = keys[:, lanes]
        attended.append(
            attend_pair(
                query[:, lanes],
                lambda q_one: jnp.where(same, mm_t(q_one, k_pair), -jnp.inf),
                values[:, lanes],
                ones,
                low,
            )
        )
    out = mm(jnp.concatenate(attended, axis=1), to_ref[...])
    out_ref[...] = (second + out).astype(BF16).reshape(nframes, count, width)


def temporal(x, w_conv, t_query, t_key, t_value, t_out, scale, block=16):
    nframes, count, width = x.shape
    weight = pl.BlockSpec((width, width), lambda i: (0, 0))
    tile = pl.BlockSpec((nframes, block, width), lambda i: (0, i, 0))
    return pl.pallas_call(
        lambda *refs: temporal_kernel(scale, *refs),
        grid=(count // block,),
        in_specs=[
            tile,
            pl.BlockSpec((3, width, width), lambda i: (0, 0, 0)),
            weight,
            weight,
            weight,
            weight,
        ],
        out_specs=tile,
        out_shape=jax.ShapeDtypeStruct(x.shape, BF16),
        compiler_params=params(),
        cost_estimate=pl.CostEstimate(
            flops=20 * nframes * count * width * width,
            bytes_accessed=2 * (2 * nframes * count * width + 7 * width * width),
            transcendentals=nframes * count * nframes * block * HEADS,
        ),
        name="temporal",
    )(x, w_conv, t_query, t_key, t_value, t_out)


def gather_rows(rows, inner=4):
    size = lax.axis_size("frame")
    outer = size // inner

    def shift(value, dy, dz):
        pairs = [
            (y * inner + z, ((y + dy) % outer) * inner + (z + dz) % inner)
            for y in range(outer)
            for z in range(inner)
        ]
        return lax.ppermute(value, "frame", pairs)

    near = jnp.concatenate([rows] + [shift(rows, 0, d) for d in range(1, inner)])
    return jnp.concatenate([near] + [shift(near, d, 0) for d in range(1, outer)])


def per_device(
    frames, ref_rows, w_query, w_key, w_value, w_out, w_conv, t_query, t_key, t_value, t_out
):
    _, pixels, width = frames.shape
    scale = LOG2E / math.sqrt(width // HEADS)
    ndev = lax.axis_size("frame")
    all_rows = gather_rows(ref_rows)
    query, kt, values = qkv(frames, w_query, w_key, w_value, scale)
    rkt, rvalues = ref_kv(all_rows, w_key, w_value)
    first = spatial(frames, query, kt, values, rkt, rvalues, w_out, 0, pixels)
    shared = lax.all_to_all(
        first.reshape(ndev, pixels // ndev, width), "frame", 0, 0, tiled=True
    )
    done = temporal(shared, w_conv, t_query, t_key, t_value, t_out, scale)
    back = lax.all_to_all(done, "frame", 0, 0, tiled=True)
    return back.reshape(1, pixels, width)


def solution(mesh):
    return jax.shard_map(
        per_device,
        mesh=mesh,
        in_specs=(P(("video", "frame"), None, None), P(("video", "frame"), None)) + (P(),) * 9,
        out_specs=P(("video", "frame"), None, None),
        check_vma=False,
    )
```

```python
import math

import jax
import jax.numpy as jnp
from jax import lax
from jax.experimental import pallas as pl
from jax.experimental.pallas import tpu as pltpu
from jax.sharding import PartitionSpec as P

HEADS = 10
LOG2E = 1.4426950408889634
BF16 = jnp.bfloat16
F32 = jnp.float32
VMEM_LIMIT = 32 * 1024 * 1024


def params():
    return pltpu.CompilerParams(vmem_limit_bytes=VMEM_LIMIT)


def shape(dims, dtype=BF16):
    return jax.ShapeDtypeStruct(dims, dtype)


def whole(a):
    return pl.BlockSpec(a.shape, lambda i: (0,) * a.ndim)


def cost(flops, nbytes, transcendentals=0):
    return pl.CostEstimate(
        flops=int(flops), bytes_accessed=int(nbytes), transcendentals=int(transcendentals)
    )


def norm_rows(value):
    mean = jnp.mean(value, axis=-1, keepdims=True)
    centered = value - mean
    var = jnp.mean(centered * centered, axis=-1, keepdims=True)
    return (centered * lax.rsqrt(var + 1e-05)).astype(BF16)


def mm(a, b):
    return jnp.dot(a, b, preferred_element_type=F32)


def mm_t(a, b):
    return lax.dot_general(a, b, (((1,), (1,)), ((), ())), preferred_element_type=F32)


def start(copies, sems):
    made = [
        pltpu.make_async_copy(source, target, sems.at[i])
        for i, (source, target) in enumerate(copies)
    ]
    for copy in made:
        copy.start()
    return made


ANY = pl.BlockSpec(memory_space=pl.ANY)


def like(a):
    return pltpu.VMEM(a.shape, a.dtype)


def in_hbm(*arrays):
    return [pltpu.with_memory_space_constraint(a, pltpu.HBM) for a in arrays]


def qkv_kernel(
    scale, x_hbm, wq_hbm, wk_hbm, wv_hbm, q_ref, kt_ref, v_ref, x_ref, wq_ref, wk_ref, wv_ref, sems
):
    pixels = x_ref.shape[0]
    half = pixels // 2
    parts = [pl.ds(0, half), pl.ds(half, half)]
    copies = [(x_hbm.at[0, parts[0]], x_ref.at[parts[0]]), (wv_hbm, wv_ref)]
    copies += [(x_hbm.at[0, parts[1]], x_ref.at[parts[1]]), (wk_hbm, wk_ref), (wq_hbm, wq_ref)]
    x0, wv, x1, wk, wq = start(copies, sems)
    x0.wait()
    low = norm_rows(x_ref[:half].astype(F32))
    wv.wait()
    v_ref[:half] = mm(low, wv_ref[...]).astype(BF16)
    x1.wait()
    high = norm_rows(x_ref[half:].astype(F32))
    v_ref[half:] = mm(high, wv_ref[...]).astype(BF16)
    wk.wait()
    kt_ref[:, :half] = mm(low, wk_ref[...]).astype(BF16).T
    kt_ref[:, half:] = mm(high, wk_ref[...]).astype(BF16).T
    wq.wait()
    q_ref[:half] = (mm(low, wq_ref[...]) * scale).astype(BF16)
    q_ref[half:] = (mm(high, wq_ref[...]) * scale).astype(BF16)


def qkv(frames, w_query, w_key, w_value, scale):
    _, pixels, width = frames.shape
    return pl.pallas_call(
        lambda *refs: qkv_kernel(scale, *refs),
        in_specs=[ANY] * 4,
        out_shape=[
            pltpu.VMEM((pixels, width), BF16),
            pltpu.VMEM((width, pixels), BF16),
            pltpu.VMEM((pixels, width), BF16),
        ],
        scratch_shapes=[pltpu.VMEM((pixels, width), BF16)]
        + [like(w) for w in (w_query, w_key, w_value)]
        + [pltpu.SemaphoreType.DMA((5,))],
        compiler_params=params(),
        cost_estimate=cost(
            6 * pixels * width * width, 2 * (4 * pixels * width + 3 * width * width)
        ),
        name="qkv",
    )(*in_hbm(frames, w_query, w_key, w_value))


def ref_kernel(x_ref, wk_ref, wv_ref, kt_ref, v_ref, kt_hbm, v_hbm, sems):
    count = x_ref.shape[0]
    half = count // 2
    copies = []
    for at, rows in enumerate((pl.ds(0, half), pl.ds(half, half))):
        v_ref[rows] = mm(x_ref[rows], wv_ref[...]).astype(BF16)
        copies += start([(v_ref.at[rows], v_hbm.at[rows])], sems.at[pl.ds(2 * at, 1)])
        kt_ref[:, rows] = mm(x_ref[rows], wk_ref[...]).astype(BF16).T
        copies += start([(kt_ref.at[:, rows], kt_hbm.at[:, rows])], sems.at[pl.ds(2 * at + 1, 1)])
    for copy in copies:
        copy.wait()


def ref_kv(rows, w_key, w_value):
    count, width = rows.shape
    return pl.pallas_call(
        ref_kernel,
        in_specs=[pl.BlockSpec(memory_space=pltpu.VMEM)] * 3,
        out_specs=[pl.BlockSpec(memory_space=pltpu.VMEM)] * 2 + [ANY] * 2,
        out_shape=[
            pltpu.VMEM((width, count), BF16),
            pltpu.VMEM((count, width), BF16),
            pltpu.HBM((width, count), BF16),
            pltpu.HBM((count, width), BF16),
        ],
        scratch_shapes=[pltpu.SemaphoreType.DMA((4,))],
        compiler_params=params(),
        cost_estimate=cost(4 * count * width * width, 2 * (3 * count * width + 2 * width * width)),
        name="ref_kv",
    )(rows, w_key, w_value)


def attend_pair(q_pair, score, values, low):
    zero = jnp.zeros_like(q_pair)
    extended = jnp.concatenate([values, jnp.ones_like(values)], axis=1)
    mixes, totals, peaks = [], [], []
    for half in range(2):
        scores = score(jnp.where(low == (half == 0), q_pair, zero))
        peak = jnp.max(scores, axis=-1, keepdims=True)
        mixed = mm(jnp.exp2(scores - peak).astype(BF16), extended)
        mixes.append(mixed[:, :128])
        totals.append(mixed[:, 128:])
        peaks.append(peak)
    return (
        jnp.where(low, mixes[0], mixes[1]),
        jnp.where(low, totals[0], totals[1]),
        jnp.where(low, peaks[0], peaks[1]),
    )


def own_kernel(q_ref, kt_ref, v_ref, mix_ref, total_ref, peak_ref):
    rows, width = mix_ref.shape
    query = q_ref[...].reshape(rows, width)
    low = lax.broadcasted_iota(jnp.int32, (rows, 128), 1) < 64
    for pair in range(width // 128):
        lanes = slice(pair * 128, pair * 128 + 128)
        mix_ref[:, lanes], total_ref[:, lanes], peak_ref[:, lanes] = attend_pair(
            query[:, lanes], lambda q_one: mm(q_one, kt_ref[lanes, :]), v_ref[:, lanes], low
        )


def attend_own(query, kt, values, part, parts, block=256):
    owners, pixels, width = query.shape
    each = pixels // parts
    count = owners * each
    keys = kt.shape[1]
    rows = pl.BlockSpec((block, width), lambda i: (i, 0))
    return pl.pallas_call(
        own_kernel,
        grid=(count // block,),
        in_specs=[
            pl.BlockSpec((block // each, each, width), lambda i: (i, part, 0)),
            whole(kt),
            whole(values),
        ],
        out_specs=[rows] * 3,
        out_shape=[pltpu.VMEM((count, width), F32)] * 3,
        compiler_params=params(),
        cost_estimate=cost(16 * count * keys * width, 18 * count * width, count * keys * HEADS),
        name="attend_own",
    )(query, kt, values)


def project_out(x_ref, attended, wo_ref, out_ref):
    out = mm(jnp.concatenate(attended, axis=1), wo_ref[...])
    x = x_ref[...].reshape(out.shape).astype(F32)
    out_ref[...] = (x + out).astype(BF16).reshape(out_ref.shape)


def ref_attend_kernel(
    x_ref, q_ref, mix_ref, total_ref, peak_ref, kt_ref, v_ref, wo_ref, out_ref
):
    rows, width = mix_ref.shape
    query = q_ref[...].reshape(rows, width)
    low = lax.broadcasted_iota(jnp.int32, (rows, 128), 1) < 64
    attended = []
    for pair in range(width // 128):
        lanes = slice(pair * 128, pair * 128 + 128)
        mix, total, peak = attend_pair(
            query[:, lanes], lambda q_one: mm(q_one, kt_ref[lanes, :]), v_ref[:, lanes], low
        )
        own_peak = peak_ref[:, lanes]
        top = jnp.maximum(peak, own_peak)
        far, near = jnp.exp2(peak - top), jnp.exp2(own_peak - top)
        mix = mix * far + mix_ref[:, lanes] * near
        total = total * far + total_ref[:, lanes] * near
        attended.append((mix / total).astype(BF16))
    project_out(x_ref, attended, wo_ref, out_ref)


def attend_ref(frames, query, own, keyed, w_out, part, parts, block=256):
    owners, pixels, width = query.shape
    each = pixels // parts
    count = owners * each
    keys = sum(a.shape[1] for a in keyed[::2])
    tile = pl.BlockSpec((block // each, each, width), lambda i: (i, part, 0))
    rows = pl.BlockSpec((block, width), lambda i: (i, 0))
    return pl.pallas_call(
        ref_attend_kernel,
        grid=(count // block,),
        in_specs=[tile, tile] + [rows] * len(own) + [whole(a) for a in (*keyed, w_out)],
        out_specs=pl.BlockSpec((block // each, each, width), lambda i: (i, 0, 0)),
        out_shape=shape((owners, each, width)),
        compiler_params=params(),
        cost_estimate=cost(16 * count * keys * width, 18 * count * width, count * keys * HEADS),
        name="attend_ref",
    )(frames, query, *own, *keyed, w_out)


def attend_kernel(
    part, x_hbm, q_hbm, kt_hbm, v_hbm, rkt_hbm, rv_hbm, wo_hbm, out_ref,
    x_ref, q_ref, kt_ref, v_ref, wo_ref, sems,
):
    owners, each, width = q_ref.shape
    keys = kt_hbm.shape[1]
    near, far = pl.ds(0, keys), pl.ds(keys, kt_ref.shape[1] - keys)
    mine = pl.ds(part * each, each)
    pairs = width // 128
    copies = []
    for pair in range(pairs):
        lanes = pl.ds(pair * 128, 128)
        copies += [
            (q_hbm.at[:, mine, lanes], q_ref.at[:, :, lanes]),
            (kt_hbm.at[lanes, :], kt_ref.at[lanes, near]),
            (rkt_hbm.at[lanes, :], kt_ref.at[lanes, far]),
            (v_hbm.at[:, lanes], v_ref.at[near, lanes]),
            (rv_hbm.at[:, lanes], v_ref.at[far, lanes]),
        ]
    copies += [(wo_hbm, wo_ref), (x_hbm.at[:, mine, :], x_ref)]
    made = start(copies, sems)
    rows = owners * each
    low = lax.broadcasted_iota(jnp.int32, (rows, 128), 1) < 64
    attended = []
    for pair in range(pairs):
        lanes = slice(pair * 128, pair * 128 + 128)
        for copy in made[5 * pair : 5 * pair + 5]:
            copy.wait()
        query = q_ref[:, :, lanes].reshape(rows, 128)
        mix, total, _ = attend_pair(
            query, lambda q_one: mm(q_one, kt_ref[lanes, :]), v_ref[:, lanes], low
        )
        attended.append((mix / total).astype(BF16))
    for copy in made[5 * pairs :]:
        copy.wait()
    project_out(x_ref, attended, wo_ref, out_ref)


def attend(frames, query, kt, values, rkt, rvalues, w_out, part, parts):
    owners, pixels, width = query.shape
    each = pixels // parts
    count = owners * each
    keys = kt.shape[1] + rkt.shape[1]
    tile = pltpu.VMEM((owners, each, width), BF16)
    return pl.pallas_call(
        lambda *refs: attend_kernel(part, *refs),
        in_specs=[ANY] * 7,
        out_shape=shape((owners, each, width)),
        scratch_shapes=[
            tile,
            tile,
            pltpu.VMEM((width, keys), BF16),
            pltpu.VMEM((keys, width), BF16),
            like(w_out),
            pltpu.SemaphoreType.DMA((5 * (width // 128) + 2,)),
        ],
        compiler_params=params(),
        cost_estimate=cost(16 * count * keys * width, 18 * count * width, count * keys * HEADS),
        name="attend",
    )(*in_hbm(frames, query, kt, values, rkt, rvalues, w_out))


def temporal_kernel(scale, group, x_ref, wc_hbm, tq_hbm, tk_hbm, tv_hbm, to_hbm, *rest):
    out_ref, wc_ref, tq_ref, tk_ref, tv_ref, to_ref, sems = rest[-7:]
    copies = [(wc_hbm.at[tap], wc_ref.at[tap]) for tap in range(3)]
    copies += [(tq_hbm, tq_ref), (tk_hbm, tk_ref), (tv_hbm, tv_ref), (to_hbm, to_ref)]
    made = start(copies, sems)
    nframes, count, width = x_ref.shape
    rows = nframes * group
    blocks = count // group
    x = jnp.concatenate(
        [x_ref[:, b * group : b * group + group, :].reshape(rows, width) for b in range(blocks)]
    )
    pad = jnp.zeros((group, width), BF16)
    before, after = [], []
    for b in range(blocks):
        one = x[b * rows : b * rows + rows]
        before += [pad, one[: rows - group]]
        after += [one[group:], pad]
    taps = (jnp.concatenate(before), x, jnp.concatenate(after))
    conv = jnp.zeros(x.shape, F32)
    for tap in range(3):
        made[tap].wait()
        conv = conv + mm(taps[tap], wc_ref[tap])
    second = (x.astype(F32) + conv).astype(BF16).astype(F32)
    normed = norm_rows(second)
    made[3].wait()
    query = (mm(normed, tq_ref[...]) * scale).astype(BF16)
    made[4].wait()
    keys = mm(normed, tk_ref[...]).astype(BF16)
    made[5].wait()
    values = mm(normed, tv_ref[...]).astype(BF16)
    low = lax.broadcasted_iota(jnp.int32, (rows, 128), 1) < 64
    mine = lax.broadcasted_iota(jnp.int32, (rows, rows), 0) % group
    theirs = lax.broadcasted_iota(jnp.int32, (rows, rows), 1) % group
    same = mine == theirs
    attended = []
    for b in range(blocks):
        here = slice(b * rows, b * rows + rows)
        pairs = []
        for pair in range(width // 128):
            lanes = slice(pair * 128, pair * 128 + 128)
            k_pair = keys[here, lanes]
            mix, total, _ = attend_pair(
                query[here, lanes],
                lambda q_one: jnp.where(same, mm_t(q_one, k_pair), -jnp.inf),
                values[here, lanes],
                low,
            )
            pairs.append((mix / total).astype(BF16))
        attended.append(jnp.concatenate(pairs, axis=1))
    made[6].wait()
    out = (second + mm(jnp.concatenate(attended), to_ref[...])).astype(BF16)
    for b in range(blocks):
        out_ref[:, b * group : b * group + group, :] = out[b * rows : b * rows + rows].reshape(
            nframes, group, width
        )


def temporal(x, weights, scale, part, parts, earlier=(), group=16):
    nframes, count, width = x.shape
    tile = (nframes, count, width)
    return pl.pallas_call(
        lambda *refs: temporal_kernel(scale, group, *refs),
        grid=(1,),
        in_specs=[pl.BlockSpec(tile, lambda i: (0, 0, 0))]
        + [ANY] * (len(weights) + len(earlier)),
        scratch_shapes=[like(w) for w in weights] + [pltpu.SemaphoreType.DMA((7,))],
        out_specs=pl.BlockSpec(tile, lambda i: (0, part, 0)),
        out_shape=shape((nframes, parts * count, width)),
        input_output_aliases={1 + len(weights): 0} if earlier else {},
        compiler_params=params(),
        cost_estimate=cost(
            30 * nframes * count * width * width,
            2 * (2 * nframes * count * width + 7 * width * width),
            nframes * count * nframes * group * HEADS,
        ),
        name="temporal",
    )(x, *in_hbm(*weights), *earlier)


def gather_rows(rows, inner=4):
    size = lax.axis_size("frame")
    outer = size // inner

    def shift(value, dy, dz):
        pairs = [
            (y * inner + z, ((y + dy) % outer) * inner + (z + dz) % inner)
            for y in range(outer)
            for z in range(inner)
        ]
        return lax.ppermute(value, "frame", pairs)

    near = jnp.concatenate([rows] + [shift(rows, 0, d) for d in range(1, inner)])
    return jnp.concatenate([near] + [shift(near, d, 0) for d in range(1, outer)])


def exchange(value):
    return lax.all_to_all(value, "frame", 0, 0, tiled=True)


def per_device(
    frames, ref_rows, w_query, w_key, w_value, w_out, w_conv, t_query, t_key, t_value, t_out
):
    _, pixels, width = frames.shape
    scale = LOG2E / math.sqrt(width // HEADS)
    ndev = lax.axis_size("frame")
    weights = (w_conv, t_query, t_key, t_value, t_out)
    all_rows = gather_rows(ref_rows)
    query, kt, values = qkv(frames, w_query, w_key, w_value, scale)
    by_owner = (ndev, pixels // ndev, width)
    frames, query = frames.reshape(by_owner), query.reshape(by_owner)
    own = attend_own(query, kt, values, 0, 2)
    rkt, rvalues, rkt_far, rvalues_far = ref_kv(all_rows, w_key, w_value)
    first = attend_ref(frames, query, own, (rkt, rvalues), w_out, 0, 2)
    first, rkt_far = lax.optimization_barrier((first, rkt_far))
    shared = exchange(first)
    other = attend(frames, query, kt, values, rkt_far, rvalues_far, w_out, 1, 2)
    other = exchange(other)
    done = temporal(shared, weights, scale, 0, 2)
    done = temporal(other, weights, scale, 1, 2, (done,))
    return exchange(done).reshape(1, pixels, width)


def solution(mesh):
    return jax.shard_map(
        per_device,
        mesh=mesh,
        in_specs=(P(("video", "frame"), None, None), P(("video", "frame"), None)) + (P(),) * 9,
        out_specs=P(("video", "frame"), None, None),
        check_vma=False,
    )
```

```python
import math

import jax
import jax.numpy as jnp
from jax import lax
from jax.experimental import pallas as pl
from jax.experimental.pallas import tpu as pltpu
from jax.sharding import PartitionSpec as P

HEADS = 10
LOG2E = 1.4426950408889634
BF16 = jnp.bfloat16
F32 = jnp.float32
VMEM_LIMIT = 32 * 1024 * 1024


def params():
    return pltpu.CompilerParams(vmem_limit_bytes=VMEM_LIMIT)


def shape(dims, dtype=BF16):
    return jax.ShapeDtypeStruct(dims, dtype)


def whole(a):
    return pl.BlockSpec(a.shape, lambda i: (0,) * a.ndim)


def cost(flops, nbytes, transcendentals=0):
    return pl.CostEstimate(
        flops=int(flops), bytes_accessed=int(nbytes), transcendentals=int(transcendentals)
    )


def norm_rows(value):
    mean = jnp.mean(value, axis=-1, keepdims=True)
    centered = value - mean
    var = jnp.mean(centered * centered, axis=-1, keepdims=True)
    return (centered * lax.rsqrt(var + 1e-05)).astype(BF16)


def mm(a, b):
    return jnp.dot(a, b, preferred_element_type=F32)


def mm_t(a, b):
    return lax.dot_general(a, b, (((1,), (1,)), ((), ())), preferred_element_type=F32)


def start(copies, sems):
    made = [
        pltpu.make_async_copy(source, target, sems.at[i])
        for i, (source, target) in enumerate(copies)
    ]
    for copy in made:
        copy.start()
    return made


ANY = pl.BlockSpec(memory_space=pl.ANY)


def like(a):
    return pltpu.VMEM(a.shape, a.dtype)


def in_hbm(*arrays):
    return [pltpu.with_memory_space_constraint(a, pltpu.HBM) for a in arrays]


def qkv_kernel(
    scale, x_hbm, wq_hbm, wk_hbm, wv_hbm, q_ref, kt_ref, v_ref, x_ref, wq_ref, wk_ref, wv_ref, sems
):
    pixels = x_ref.shape[0]
    half = pixels // 2
    parts = [pl.ds(0, half), pl.ds(half, half)]
    copies = [(x_hbm.at[0, parts[0]], x_ref.at[parts[0]]), (wv_hbm, wv_ref)]
    copies += [(x_hbm.at[0, parts[1]], x_ref.at[parts[1]]), (wk_hbm, wk_ref), (wq_hbm, wq_ref)]
    x0, wv, x1, wk, wq = start(copies, sems)
    x0.wait()
    low = norm_rows(x_ref[:half].astype(F32))
    wv.wait()
    v_ref[:half] = mm(low, wv_ref[...]).astype(BF16)
    x1.wait()
    high = norm_rows(x_ref[half:].astype(F32))
    v_ref[half:] = mm(high, wv_ref[...]).astype(BF16)
    wk.wait()
    kt_ref[:, :half] = mm(low, wk_ref[...]).astype(BF16).T
    kt_ref[:, half:] = mm(high, wk_ref[...]).astype(BF16).T
    wq.wait()
    q_ref[:half] = (mm(low, wq_ref[...]) * scale).astype(BF16)
    q_ref[half:] = (mm(high, wq_ref[...]) * scale).astype(BF16)


def qkv(frames, w_query, w_key, w_value, scale):
    _, pixels, width = frames.shape
    return pl.pallas_call(
        lambda *refs: qkv_kernel(scale, *refs),
        in_specs=[ANY] * 4,
        out_shape=[
            pltpu.VMEM((pixels, width), BF16),
            pltpu.VMEM((width, pixels), BF16),
            pltpu.VMEM((pixels, width), BF16),
        ],
        scratch_shapes=[pltpu.VMEM((pixels, width), BF16)]
        + [like(w) for w in (w_query, w_key, w_value)]
        + [pltpu.SemaphoreType.DMA((5,))],
        compiler_params=params(),
        cost_estimate=cost(
            6 * pixels * width * width, 2 * (4 * pixels * width + 3 * width * width)
        ),
        name="qkv",
    )(*in_hbm(frames, w_query, w_key, w_value))


def ref_kernel(x_ref, wk_ref, wv_ref, kt_ref, v_ref):
    kt_ref[...] = mm(x_ref[...], wk_ref[...]).astype(BF16).T
    v_ref[...] = mm(x_ref[...], wv_ref[...]).astype(BF16)


def ref_kv(rows, w_key, w_value, block=256):
    count, width = rows.shape
    spec = pl.BlockSpec((block, width), lambda i: (i, 0))
    return pl.pallas_call(
        ref_kernel,
        grid=(count // block,),
        in_specs=[spec, whole(w_key), whole(w_value)],
        out_specs=[pl.BlockSpec((width, block), lambda i: (0, i)), spec],
        out_shape=[pltpu.VMEM((width, count), BF16), pltpu.VMEM((count, width), BF16)],
        compiler_params=params(),
        cost_estimate=cost(4 * count * width * width, 2 * (3 * count * width + 2 * width * width)),
        name="ref_kv",
    )(rows, w_key, w_value)


def attend_pair(q_pair, score, values, low):
    zero = jnp.zeros_like(q_pair)
    extended = jnp.concatenate([values, jnp.ones_like(values)], axis=1)
    mixes, totals, peaks = [], [], []
    for half in range(2):
        scores = score(jnp.where(low == (half == 0), q_pair, zero))
        peak = jnp.max(scores, axis=-1, keepdims=True)
        mixed = mm(jnp.exp2(scores - peak).astype(BF16), extended)
        mixes.append(mixed[:, :128])
        totals.append(mixed[:, 128:])
        peaks.append(peak)
    return (
        jnp.where(low, mixes[0], mixes[1]),
        jnp.where(low, totals[0], totals[1]),
        jnp.where(low, peaks[0], peaks[1]),
    )


def own_kernel(q_ref, kt_ref, v_ref, mix_ref, total_ref, peak_ref):
    rows, width = mix_ref.shape
    low = lax.broadcasted_iota(jnp.int32, (rows, 128), 1) < 64
    for pair in range(width // 128):
        lanes = slice(pair * 128, pair * 128 + 128)
        mix_ref[:, lanes], total_ref[:, lanes], peak_ref[:, lanes] = attend_pair(
            q_ref[:, lanes], lambda q_one: mm(q_one, kt_ref[lanes, :]), v_ref[:, lanes], low
        )


def attend_own(query, kt, values, block=256):
    pixels, width = query.shape
    rows = pl.BlockSpec((block, width), lambda i: (i, 0))
    return pl.pallas_call(
        own_kernel,
        grid=(pixels // block,),
        in_specs=[rows, whole(kt), whole(values)],
        out_specs=[rows] * 3,
        out_shape=[pltpu.VMEM((pixels, width), F32)] * 3,
        compiler_params=params(),
        cost_estimate=cost(
            16 * pixels * pixels * width, 18 * pixels * width, pixels * pixels * HEADS
        ),
        name="attend_own",
    )(query, kt, values)


def ref_attend_kernel(
    x_ref, q_ref, mix_ref, total_ref, peak_ref, kt_ref, v_ref, wo_ref, out_ref
):
    rows, width = mix_ref.shape
    low = lax.broadcasted_iota(jnp.int32, (rows, 128), 1) < 64
    attended = []
    for pair in range(width // 128):
        lanes = slice(pair * 128, pair * 128 + 128)
        mix, total, peak = attend_pair(
            q_ref[:, lanes], lambda q_one: mm(q_one, kt_ref[lanes, :]), v_ref[:, lanes], low
        )
        own_peak = peak_ref[:, lanes]
        top = jnp.maximum(peak, own_peak)
        far, near = jnp.exp2(peak - top), jnp.exp2(own_peak - top)
        mix = mix * far + mix_ref[:, lanes] * near
        total = total * far + total_ref[:, lanes] * near
        attended.append((mix / total).astype(BF16))
    out = mm(jnp.concatenate(attended, axis=1), wo_ref[...])
    out_ref[...] = (x_ref[0].astype(F32) + out).astype(BF16)


def attend_ref(frames, query, own, kt, values, w_out, block=256):
    pixels, width = query.shape
    keys = kt.shape[1]
    rows = pl.BlockSpec((block, width), lambda i: (i, 0))
    return pl.pallas_call(
        ref_attend_kernel,
        grid=(pixels // block,),
        in_specs=[pl.BlockSpec((1, block, width), lambda i: (0, i, 0))]
        + [rows] * 4
        + [whole(kt), whole(values), whole(w_out)],
        out_specs=rows,
        out_shape=shape((pixels, width)),
        compiler_params=params(),
        cost_estimate=cost(
            16 * pixels * keys * width, 18 * pixels * width, pixels * keys * HEADS
        ),
        name="attend_ref",
    )(frames, query, *own, kt, values, w_out)


def temporal_kernel(scale, group, x_ref, wc_ref, tq_ref, tk_ref, tv_ref, to_ref, out_ref):
    nframes, count, width = x_ref.shape
    rows = nframes * group
    blocks = count // group
    x = jnp.concatenate(
        [x_ref[:, b * group : b * group + group, :].reshape(rows, width) for b in range(blocks)]
    )
    pad = jnp.zeros((group, width), BF16)
    before, after = [], []
    for b in range(blocks):
        one = x[b * rows : b * rows + rows]
        before += [pad, one[: rows - group]]
        after += [one[group:], pad]
    taps = jnp.concatenate([jnp.concatenate(before), x, jnp.concatenate(after)], axis=1)
    conv = mm(taps, wc_ref[...].reshape(3 * width, width))
    second = (x.astype(F32) + conv).astype(BF16).astype(F32)
    normed = norm_rows(second)
    query = (mm(normed, tq_ref[...]) * scale).astype(BF16)
    keys = mm(normed, tk_ref[...]).astype(BF16)
    values = mm(normed, tv_ref[...]).astype(BF16)
    low = lax.broadcasted_iota(jnp.int32, (rows, 128), 1) < 64
    mine = lax.broadcasted_iota(jnp.int32, (rows, rows), 0) % group
    theirs = lax.broadcasted_iota(jnp.int32, (rows, rows), 1) % group
    same = mine == theirs
    attended = []
    for b in range(blocks):
        here = slice(b * rows, b * rows + rows)
        pairs = []
        for pair in range(width // 128):
            lanes = slice(pair * 128, pair * 128 + 128)
            k_pair = keys[here, lanes]
            mix, total, _ = attend_pair(
                query[here, lanes],
                lambda q_one: jnp.where(same, mm_t(q_one, k_pair), -jnp.inf),
                values[here, lanes],
                low,
            )
            pairs.append((mix / total).astype(BF16))
        attended.append(jnp.concatenate(pairs, axis=1))
    out = (second + mm(jnp.concatenate(attended), to_ref[...])).astype(BF16)
    for b in range(blocks):
        out_ref[:, b * group : b * group + group, :] = out[b * rows : b * rows + rows].reshape(
            nframes, group, width
        )


def temporal(x, weights, scale, block=16, group=16):
    nframes, count, width = x.shape
    tile = pl.BlockSpec((nframes, block, width), lambda i: (0, i, 0))
    return pl.pallas_call(
        lambda *refs: temporal_kernel(scale, group, *refs),
        grid=(count // block,),
        in_specs=[tile] + [whole(w) for w in weights],
        out_specs=tile,
        out_shape=shape(x.shape),
        compiler_params=params(),
        cost_estimate=cost(
            30 * nframes * count * width * width,
            2 * (2 * nframes * count * width + 7 * width * width),
            nframes * count * nframes * group * HEADS,
        ),
        name="temporal",
    )(x, *weights)


def gather_rows(rows, inner=4):
    size = lax.axis_size("frame")
    outer = size // inner

    def shift(value, dy, dz):
        pairs = [
            (y * inner + z, ((y + dy) % outer) * inner + (z + dz) % inner)
            for y in range(outer)
            for z in range(inner)
        ]
        return lax.ppermute(value, "frame", pairs)

    near = jnp.concatenate([rows] + [shift(rows, 0, d) for d in range(1, inner)])
    return jnp.concatenate([near] + [shift(near, d, 0) for d in range(1, outer)])


def exchange(value):
    return lax.all_to_all(value, "frame", 0, 0, tiled=True)


def per_device(
    frames, ref_rows, w_query, w_key, w_value, w_out, w_conv, t_query, t_key, t_value, t_out
):
    _, pixels, width = frames.shape
    scale = LOG2E / math.sqrt(width // HEADS)
    ndev = lax.axis_size("frame")
    weights = (w_conv, t_query, t_key, t_value, t_out)
    all_rows = gather_rows(ref_rows)
    query, kt, values = qkv(frames, w_query, w_key, w_value, scale)
    own = attend_own(query, kt, values)
    rkt, rvalues = ref_kv(all_rows, w_key, w_value)
    first = attend_ref(frames, query, own, rkt, rvalues, w_out)
    shared = exchange(first.reshape(ndev, pixels // ndev, width))
    done = temporal(shared, weights, scale)
    return exchange(done).reshape(1, pixels, width)


def solution(mesh):
    return jax.shard_map(
        per_device,
        mesh=mesh,
        in_specs=(P(("video", "frame"), None, None), P(("video", "frame"), None)) + (P(),) * 9,
        out_specs=P(("video", "frame"), None, None),
        check_vma=False,
    )
```

```python
import math

import jax
import jax.numpy as jnp
from jax import lax
from jax.experimental import pallas as pl
from jax.experimental.pallas import tpu as pltpu
from jax.sharding import PartitionSpec as P

HEADS = 10
LOG2E = 1.4426950408889634
BF16 = jnp.bfloat16
F32 = jnp.float32
VMEM_LIMIT = 32 * 1024 * 1024


def params():
    return pltpu.CompilerParams(vmem_limit_bytes=VMEM_LIMIT)


def shape(dims, dtype=BF16):
    return jax.ShapeDtypeStruct(dims, dtype)


def whole(a):
    return pl.BlockSpec(a.shape, lambda i: (0,) * a.ndim)


def cost(flops, nbytes, transcendentals=0):
    return pl.CostEstimate(
        flops=int(flops), bytes_accessed=int(nbytes), transcendentals=int(transcendentals)
    )


def norm_rows(value):
    mean = jnp.mean(value, axis=-1, keepdims=True)
    centered = value - mean
    var = jnp.mean(centered * centered, axis=-1, keepdims=True)
    return (centered * lax.rsqrt(var + 1e-05)).astype(BF16)


def mm(a, b):
    return jnp.dot(a, b, preferred_element_type=F32)


def mm_t(a, b):
    return lax.dot_general(a, b, (((1,), (1,)), ((), ())), preferred_element_type=F32)


def start(copies, sems):
    made = [
        pltpu.make_async_copy(source, target, sems.at[i])
        for i, (source, target) in enumerate(copies)
    ]
    for copy in made:
        copy.start()
    return made


ANY = pl.BlockSpec(memory_space=pl.ANY)


def like(a):
    return pltpu.VMEM(a.shape, a.dtype)


def in_hbm(*arrays):
    return [pltpu.with_memory_space_constraint(a, pltpu.HBM) for a in arrays]


def qkv_kernel(
    scale, x_hbm, wq_hbm, wk_hbm, wv_hbm, q_ref, kt_ref, v_ref, wk_ref, wv_ref, x_ref, wq_ref, sems
):
    pixels = x_ref.shape[0]
    half = pixels // 2
    parts = [pl.ds(0, half), pl.ds(half, half)]
    copies = [(x_hbm.at[0, parts[0]], x_ref.at[parts[0]]), (wv_hbm, wv_ref)]
    copies += [(x_hbm.at[0, parts[1]], x_ref.at[parts[1]]), (wk_hbm, wk_ref), (wq_hbm, wq_ref)]
    x0, wv, x1, wk, wq = start(copies, sems)
    x0.wait()
    low = norm_rows(x_ref[:half].astype(F32))
    wv.wait()
    v_ref[:half] = mm(low, wv_ref[...]).astype(BF16)
    x1.wait()
    high = norm_rows(x_ref[half:].astype(F32))
    v_ref[half:] = mm(high, wv_ref[...]).astype(BF16)
    wk.wait()
    kt_ref[:, :half] = mm(low, wk_ref[...]).astype(BF16).T
    kt_ref[:, half:] = mm(high, wk_ref[...]).astype(BF16).T
    wq.wait()
    q_ref[:half] = (mm(low, wq_ref[...]) * scale).astype(BF16)
    q_ref[half:] = (mm(high, wq_ref[...]) * scale).astype(BF16)


def qkv(frames, w_query, w_key, w_value, scale):
    _, pixels, width = frames.shape
    return pl.pallas_call(
        lambda *refs: qkv_kernel(scale, *refs),
        in_specs=[ANY] * 4,
        out_shape=[
            pltpu.VMEM((pixels, width), BF16),
            pltpu.VMEM((width, pixels), BF16),
            pltpu.VMEM((pixels, width), BF16),
            like(w_key),
            like(w_value),
        ],
        scratch_shapes=[
            pltpu.VMEM((pixels, width), BF16),
            like(w_query),
            pltpu.SemaphoreType.DMA((5,)),
        ],
        compiler_params=params(),
        cost_estimate=cost(
            6 * pixels * width * width, 2 * (4 * pixels * width + 3 * width * width)
        ),
        name="qkv",
    )(*in_hbm(frames, w_query, w_key, w_value))


def ref_kernel(x_ref, wk_ref, wv_ref, kt_ref, v_ref):
    kt_ref[...] = mm(x_ref[...], wk_ref[...]).astype(BF16).T
    v_ref[...] = mm(x_ref[...], wv_ref[...]).astype(BF16)


def ref_kv(rows, w_key, w_value, block=256):
    count, width = rows.shape
    spec = pl.BlockSpec((block, width), lambda i: (i, 0))
    return pl.pallas_call(
        ref_kernel,
        grid=(count // block,),
        in_specs=[spec, whole(w_key), whole(w_value)],
        out_specs=[pl.BlockSpec((width, block), lambda i: (0, i)), spec],
        out_shape=[pltpu.VMEM((width, count), BF16), pltpu.VMEM((count, width), BF16)],
        compiler_params=params(),
        cost_estimate=cost(4 * count * width * width, 2 * (3 * count * width + 2 * width * width)),
        name="ref_kv",
    )(rows, w_key, w_value)


def attend_pair(q_pair, score, values, low):
    zero = jnp.zeros_like(q_pair)
    extended = jnp.concatenate([values, jnp.ones_like(values)], axis=1)
    mixes, totals, peaks = [], [], []
    for half in range(2):
        scores = score(jnp.where(low == (half == 0), q_pair, zero))
        peak = jnp.max(scores, axis=-1, keepdims=True)
        mixed = mm(jnp.exp2(scores - peak).astype(BF16), extended)
        mixes.append(mixed[:, :128])
        totals.append(mixed[:, 128:])
        peaks.append(peak)
    return (
        jnp.where(low, mixes[0], mixes[1]),
        jnp.where(low, totals[0], totals[1]),
        jnp.where(low, peaks[0], peaks[1]),
    )


def own_kernel(q_ref, kt_ref, v_ref, mix_ref, total_ref, peak_ref):
    rows, width = mix_ref.shape
    low = lax.broadcasted_iota(jnp.int32, (rows, 128), 1) < 64
    for pair in range(width // 128):
        lanes = slice(pair * 128, pair * 128 + 128)
        mix_ref[:, lanes], total_ref[:, lanes], peak_ref[:, lanes] = attend_pair(
            q_ref[:, lanes], lambda q_one: mm(q_one, kt_ref[lanes, :]), v_ref[:, lanes], low
        )


def attend_own(query, kt, values, block=512):
    pixels, width = query.shape
    rows = pl.BlockSpec((block, width), lambda i: (i, 0))
    return pl.pallas_call(
        own_kernel,
        grid=(pixels // block,),
        in_specs=[rows, whole(kt), whole(values)],
        out_specs=[rows] * 3,
        out_shape=[pltpu.VMEM((pixels, width), F32)] * 3,
        compiler_params=params(),
        cost_estimate=cost(
            16 * pixels * pixels * width, 18 * pixels * width, pixels * pixels * HEADS
        ),
        name="attend_own",
    )(query, kt, values)


def ref_attend_kernel(
    x_ref, q_ref, mix_ref, total_ref, peak_ref, kt_ref, v_ref, wo_ref, out_ref
):
    rows, width = mix_ref.shape
    low = lax.broadcasted_iota(jnp.int32, (rows, 128), 1) < 64
    attended = []
    for pair in range(width // 128):
        lanes = slice(pair * 128, pair * 128 + 128)
        mix, total, peak = attend_pair(
            q_ref[:, lanes], lambda q_one: mm(q_one, kt_ref[lanes, :]), v_ref[:, lanes], low
        )
        own_peak = peak_ref[:, lanes]
        top = jnp.maximum(peak, own_peak)
        far, near = jnp.exp2(peak - top), jnp.exp2(own_peak - top)
        mix = mix * far + mix_ref[:, lanes] * near
        total = total * far + total_ref[:, lanes] * near
        attended.append((mix / total).astype(BF16))
    out = mm(jnp.concatenate(attended, axis=1), wo_ref[...])
    out_ref[...] = (x_ref[0].astype(F32) + out).astype(BF16)


def attend_ref(frames, query, own, kt, values, w_out, block=512):
    pixels, width = query.shape
    keys = kt.shape[1]
    rows = pl.BlockSpec((block, width), lambda i: (i, 0))
    return pl.pallas_call(
        ref_attend_kernel,
        grid=(pixels // block,),
        in_specs=[pl.BlockSpec((1, block, width), lambda i: (0, i, 0))]
        + [rows] * 4
        + [whole(kt), whole(values), whole(w_out)],
        out_specs=rows,
        out_shape=shape((pixels, width)),
        compiler_params=params(),
        cost_estimate=cost(
            16 * pixels * keys * width, 18 * pixels * width, pixels * keys * HEADS
        ),
        name="attend_ref",
    )(frames, query, *own, kt, values, w_out)


def temporal_kernel(scale, group, x_ref, wc_ref, tq_ref, tk_ref, tv_ref, to_ref, out_ref):
    nframes, count, width = x_ref.shape
    rows = nframes * group
    blocks = count // group
    x = jnp.concatenate(
        [x_ref[:, b * group : b * group + group, :].reshape(rows, width) for b in range(blocks)]
    )
    pad = jnp.zeros((group, width), BF16)
    before, after = [], []
    for b in range(blocks):
        one = x[b * rows : b * rows + rows]
        before += [pad, one[: rows - group]]
        after += [one[group:], pad]
    taps = jnp.concatenate([jnp.concatenate(before), x, jnp.concatenate(after)], axis=1)
    conv = mm(taps, wc_ref[...].reshape(3 * width, width))
    second = (x.astype(F32) + conv).astype(BF16).astype(F32)
    normed = norm_rows(second)
    query = (mm(normed, tq_ref[...]) * scale).astype(BF16)
    keys = mm(normed, tk_ref[...]).astype(BF16)
    values = mm(normed, tv_ref[...]).astype(BF16)
    low = lax.broadcasted_iota(jnp.int32, (rows, 128), 1) < 64
    mine = lax.broadcasted_iota(jnp.int32, (rows, rows), 0) % group
    theirs = lax.broadcasted_iota(jnp.int32, (rows, rows), 1) % group
    same = mine == theirs
    attended = []
    for b in range(blocks):
        here = slice(b * rows, b * rows + rows)
        pairs = []
        for pair in range(width // 128):
            lanes = slice(pair * 128, pair * 128 + 128)
            k_pair = keys[here, lanes]
            mix, total, _ = attend_pair(
                query[here, lanes],
                lambda q_one: jnp.where(same, mm_t(q_one, k_pair), -jnp.inf),
                values[here, lanes],
                low,
            )
            pairs.append((mix / total).astype(BF16))
        attended.append(jnp.concatenate(pairs, axis=1))
    out = (second + mm(jnp.concatenate(attended), to_ref[...])).astype(BF16)
    for b in range(blocks):
        out_ref[:, b * group : b * group + group, :] = out[b * rows : b * rows + rows].reshape(
            nframes, group, width
        )


def temporal(x, weights, scale, block=64, group=16):
    nframes, count, width = x.shape
    tile = pl.BlockSpec((nframes, block, width), lambda i: (0, i, 0))
    return pl.pallas_call(
        lambda *refs: temporal_kernel(scale, group, *refs),
        grid=(count // block,),
        in_specs=[tile] + [whole(w) for w in weights],
        out_specs=tile,
        out_shape=shape(x.shape),
        compiler_params=params(),
        cost_estimate=cost(
            30 * nframes * count * width * width,
            2 * (2 * nframes * count * width + 7 * width * width),
            nframes * count * nframes * group * HEADS,
        ),
        name="temporal",
    )(x, *weights)


def gather_rows(rows, inner=4):
    size = lax.axis_size("frame")
    outer = size // inner

    def shift(value, dy, dz):
        pairs = [
            (y * inner + z, ((y + dy) % outer) * inner + (z + dz) % inner)
            for y in range(outer)
            for z in range(inner)
        ]
        return lax.ppermute(value, "frame", pairs)

    near = jnp.concatenate([rows] + [shift(rows, 0, d) for d in range(1, inner)])
    return jnp.concatenate([near] + [shift(near, d, 0) for d in range(1, outer)])


def exchange(value):
    return lax.all_to_all(value, "frame", 0, 0, tiled=True)


def per_device(
    frames, ref_rows, w_query, w_key, w_value, w_out, w_conv, t_query, t_key, t_value, t_out
):
    _, pixels, width = frames.shape
    scale = LOG2E / math.sqrt(width // HEADS)
    ndev = lax.axis_size("frame")
    weights = (w_conv, t_query, t_key, t_value, t_out)
    all_rows = gather_rows(ref_rows)
    query, kt, values, near_key, near_value = qkv(frames, w_query, w_key, w_value, scale)
    own = attend_own(query, kt, values)
    rkt, rvalues = ref_kv(all_rows, near_key, near_value)
    first = attend_ref(frames, query, own, rkt, rvalues, w_out)
    shared = exchange(first.reshape(ndev, pixels // ndev, width))
    done = temporal(shared, weights, scale)
    return exchange(done).reshape(1, pixels, width)


def solution(mesh):
    return jax.shard_map(
        per_device,
        mesh=mesh,
        in_specs=(P(("video", "frame"), None, None), P(("video", "frame"), None)) + (P(),) * 9,
        out_specs=P(("video", "frame"), None, None),
        check_vma=False,
    )
```

```python
import math

import jax
import jax.numpy as jnp
from jax import lax
from jax.experimental import pallas as pl
from jax.experimental.pallas import tpu as pltpu
from jax.sharding import PartitionSpec as P

HEADS = 10
LOG2E = 1.4426950408889634
BF16 = jnp.bfloat16
F32 = jnp.float32
VMEM_LIMIT = 32 * 1024 * 1024


def params():
    return pltpu.CompilerParams(vmem_limit_bytes=VMEM_LIMIT)


def shape(dims, dtype=BF16):
    return jax.ShapeDtypeStruct(dims, dtype)


def whole(a):
    return pl.BlockSpec(a.shape, lambda i: (0,) * a.ndim)


def cost(flops, nbytes, transcendentals=0):
    return pl.CostEstimate(
        flops=int(flops), bytes_accessed=int(nbytes), transcendentals=int(transcendentals)
    )


def norm_rows(value):
    mean = jnp.mean(value, axis=-1, keepdims=True)
    centered = value - mean
    var = jnp.mean(centered * centered, axis=-1, keepdims=True)
    return (centered * lax.rsqrt(var + 1e-05)).astype(BF16)


def mm(a, b):
    return jnp.dot(a, b, preferred_element_type=F32)


def mm_t(a, b):
    return lax.dot_general(a, b, (((1,), (1,)), ((), ())), preferred_element_type=F32)


def start(copies, sems):
    made = [
        pltpu.make_async_copy(source, target, sems.at[i])
        for i, (source, target) in enumerate(copies)
    ]
    for copy in made:
        copy.start()
    return made


ANY = pl.BlockSpec(memory_space=pl.ANY)


def like(a):
    return pltpu.VMEM(a.shape, a.dtype)


def in_hbm(*arrays):
    return [pltpu.with_memory_space_constraint(a, pltpu.HBM) for a in arrays]


def qkv_kernel(
    scale, x_hbm, wq_hbm, wk_hbm, wv_hbm, q_ref, kt_ref, v_ref, wk_ref, wv_ref, x_ref, wq_ref, sems
):
    pixels = x_ref.shape[0]
    half = pixels // 2
    parts = [pl.ds(0, half), pl.ds(half, half)]
    copies = [(x_hbm.at[0, parts[0]], x_ref.at[parts[0]]), (wv_hbm, wv_ref)]
    copies += [(x_hbm.at[0, parts[1]], x_ref.at[parts[1]]), (wk_hbm, wk_ref), (wq_hbm, wq_ref)]
    x0, wv, x1, wk, wq = start(copies, sems)
    x0.wait()
    low = norm_rows(x_ref[:half].astype(F32))
    wv.wait()
    v_ref[:half] = mm(low, wv_ref[...]).astype(BF16)
    x1.wait()
    high = norm_rows(x_ref[half:].astype(F32))
    v_ref[half:] = mm(high, wv_ref[...]).astype(BF16)
    wk.wait()
    kt_ref[:, :half] = mm(low, wk_ref[...]).astype(BF16).T
    kt_ref[:, half:] = mm(high, wk_ref[...]).astype(BF16).T
    wq.wait()
    q_ref[:half] = (mm(low, wq_ref[...]) * scale).astype(BF16)
    q_ref[half:] = (mm(high, wq_ref[...]) * scale).astype(BF16)


def qkv(frames, w_query, w_key, w_value, scale):
    _, pixels, width = frames.shape
    return pl.pallas_call(
        lambda *refs: qkv_kernel(scale, *refs),
        in_specs=[ANY] * 4,
        out_shape=[
            pltpu.VMEM((pixels, width), BF16),
            pltpu.VMEM((width, pixels), BF16),
            pltpu.VMEM((pixels, width), BF16),
            like(w_key),
            like(w_value),
        ],
        scratch_shapes=[
            pltpu.VMEM((pixels, width), BF16),
            like(w_query),
            pltpu.SemaphoreType.DMA((5,)),
        ],
        compiler_params=params(),
        cost_estimate=cost(
            6 * pixels * width * width, 2 * (4 * pixels * width + 3 * width * width)
        ),
        name="qkv",
    )(*in_hbm(frames, w_query, w_key, w_value))


def ref_kernel(x_ref, wk_ref, wv_ref, kt_ref, v_ref):
    kt_ref[...] = mm(x_ref[...], wk_ref[...]).astype(BF16).T
    v_ref[...] = mm(x_ref[...], wv_ref[...]).astype(BF16)


def ref_kv(rows, w_key, w_value, block=256):
    count, width = rows.shape
    spec = pl.BlockSpec((block, width), lambda i: (i, 0))
    return pl.pallas_call(
        ref_kernel,
        grid=(count // block,),
        in_specs=[spec, whole(w_key), whole(w_value)],
        out_specs=[pl.BlockSpec((width, block), lambda i: (0, i)), spec],
        out_shape=[pltpu.VMEM((width, count), BF16), pltpu.VMEM((count, width), BF16)],
        compiler_params=params(),
        cost_estimate=cost(4 * count * width * width, 2 * (3 * count * width + 2 * width * width)),
        name="ref_kv",
    )(rows, w_key, w_value)


def attend_pair(q_pair, score, values, low):
    zero = jnp.zeros_like(q_pair)
    extended = jnp.concatenate([values, jnp.ones_like(values)], axis=1)
    mixes, totals, peaks = [], [], []
    for half in range(2):
        scores = score(jnp.where(low == (half == 0), q_pair, zero))
        peak = jnp.max(scores, axis=-1, keepdims=True)
        mixed = mm(jnp.exp2(scores - peak).astype(BF16), extended)
        mixes.append(mixed[:, :128])
        totals.append(mixed[:, 128:])
        peaks.append(peak)
    return (
        jnp.where(low, mixes[0], mixes[1]),
        jnp.where(low, totals[0], totals[1]),
        jnp.where(low, peaks[0], peaks[1]),
    )


def own_kernel(q_ref, kt_ref, v_ref, mix_ref, total_ref, peak_ref):
    rows, width = mix_ref.shape
    low = lax.broadcasted_iota(jnp.int32, (rows, 128), 1) < 64
    for pair in range(width // 128):
        lanes = slice(pair * 128, pair * 128 + 128)
        mix_ref[:, lanes], total_ref[:, lanes], peak_ref[:, lanes] = attend_pair(
            q_ref[:, lanes], lambda q_one: mm(q_one, kt_ref[lanes, :]), v_ref[:, lanes], low
        )


def attend_own(query, kt, values, block=512):
    pixels, width = query.shape
    rows = pl.BlockSpec((block, width), lambda i: (i, 0))
    return pl.pallas_call(
        own_kernel,
        grid=(pixels // block,),
        in_specs=[rows, whole(kt), whole(values)],
        out_specs=[rows] * 3,
        out_shape=[pltpu.VMEM((pixels, width), F32)] * 3,
        compiler_params=params(),
        cost_estimate=cost(
            16 * pixels * pixels * width, 18 * pixels * width, pixels * pixels * HEADS
        ),
        name="attend_own",
    )(query, kt, values)


def ref_attend_kernel(x_ref, q_ref, mix_ref, total_ref, peak_ref, *refs):
    pieces, (wo_ref, out_ref) = refs[:-2], refs[-2:]
    rows, width = mix_ref.shape
    low = lax.broadcasted_iota(jnp.int32, (rows, 128), 1) < 64
    attended = []
    for pair in range(width // 128):
        lanes = slice(pair * 128, pair * 128 + 128)
        kt = jnp.concatenate([ref[lanes, :] for ref in pieces[::2]], axis=1)
        values = jnp.concatenate([ref[:, lanes] for ref in pieces[1::2]], axis=0)
        mix, total, peak = attend_pair(
            q_ref[:, lanes], lambda q_one: mm(q_one, kt), values, low
        )
        own_peak = peak_ref[:, lanes]
        top = jnp.maximum(peak, own_peak)
        far, near = jnp.exp2(peak - top), jnp.exp2(own_peak - top)
        mix = mix * far + mix_ref[:, lanes] * near
        total = total * far + total_ref[:, lanes] * near
        attended.append((mix / total).astype(BF16))
    out = mm(jnp.concatenate(attended, axis=1), wo_ref[...])
    out_ref[...] = (x_ref[0].astype(F32) + out).astype(BF16)


def attend_ref(frames, query, own, pieces, w_out, block=512):
    pixels, width = query.shape
    keys = sum(piece.shape[1] for piece in pieces[::2])
    rows = pl.BlockSpec((block, width), lambda i: (i, 0))
    return pl.pallas_call(
        ref_attend_kernel,
        grid=(pixels // block,),
        in_specs=[pl.BlockSpec((1, block, width), lambda i: (0, i, 0))]
        + [rows] * 4
        + [whole(a) for a in (*pieces, w_out)],
        out_specs=rows,
        out_shape=shape((pixels, width)),
        compiler_params=params(),
        cost_estimate=cost(
            16 * pixels * keys * width, 18 * pixels * width, pixels * keys * HEADS
        ),
        name="attend_ref",
    )(frames, query, *own, *pieces, w_out)


def temporal_kernel(scale, group, x_ref, wc_ref, tq_ref, tk_ref, tv_ref, to_ref, out_ref):
    nframes, count, width = x_ref.shape
    rows = nframes * group
    blocks = count // group
    x = jnp.concatenate(
        [x_ref[:, b * group : b * group + group, :].reshape(rows, width) for b in range(blocks)]
    )
    pad = jnp.zeros((group, width), BF16)
    before, after = [], []
    for b in range(blocks):
        one = x[b * rows : b * rows + rows]
        before += [pad, one[: rows - group]]
        after += [one[group:], pad]
    taps = jnp.concatenate([jnp.concatenate(before), x, jnp.concatenate(after)], axis=1)
    conv = mm(taps, wc_ref[...].reshape(3 * width, width))
    second = (x.astype(F32) + conv).astype(BF16).astype(F32)
    normed = norm_rows(second)
    query = (mm(normed, tq_ref[...]) * scale).astype(BF16)
    keys = mm(normed, tk_ref[...]).astype(BF16)
    values = mm(normed, tv_ref[...]).astype(BF16)
    low = lax.broadcasted_iota(jnp.int32, (rows, 128), 1) < 64
    mine = lax.broadcasted_iota(jnp.int32, (rows, rows), 0) % group
    theirs = lax.broadcasted_iota(jnp.int32, (rows, rows), 1) % group
    same = mine == theirs
    attended = []
    for b in range(blocks):
        here = slice(b * rows, b * rows + rows)
        pairs = []
        for pair in range(width // 128):
            lanes = slice(pair * 128, pair * 128 + 128)
            k_pair = keys[here, lanes]
            mix, total, _ = attend_pair(
                query[here, lanes],
                lambda q_one: jnp.where(same, mm_t(q_one, k_pair), -jnp.inf),
                values[here, lanes],
                low,
            )
            pairs.append((mix / total).astype(BF16))
        attended.append(jnp.concatenate(pairs, axis=1))
    out = (second + mm(jnp.concatenate(attended), to_ref[...])).astype(BF16)
    for b in range(blocks):
        out_ref[:, b * group : b * group + group, :] = out[b * rows : b * rows + rows].reshape(
            nframes, group, width
        )


def temporal(x, weights, scale, block=64, group=16):
    nframes, count, width = x.shape
    tile = pl.BlockSpec((nframes, block, width), lambda i: (0, i, 0))
    return pl.pallas_call(
        lambda *refs: temporal_kernel(scale, group, *refs),
        grid=(count // block,),
        in_specs=[tile] + [whole(w) for w in weights],
        out_specs=tile,
        out_shape=shape(x.shape),
        compiler_params=params(),
        cost_estimate=cost(
            30 * nframes * count * width * width,
            2 * (2 * nframes * count * width + 7 * width * width),
            nframes * count * nframes * group * HEADS,
        ),
        name="temporal",
    )(x, *weights)


def gather_rows(rows, inner=4):
    size = lax.axis_size("frame")
    outer = size // inner

    def shift(value, dy, dz):
        pairs = [
            (y * inner + z, ((y + dy) % outer) * inner + (z + dz) % inner)
            for y in range(outer)
            for z in range(inner)
        ]
        return lax.ppermute(value, "frame", pairs)

    near = jnp.concatenate([rows] + [shift(rows, 0, d) for d in range(1, inner)])
    return [near] + [shift(near, d, 0) for d in range(1, outer)]


def exchange(value):
    return lax.all_to_all(value, "frame", 0, 0, tiled=True)


def per_device(
    frames, ref_rows, w_query, w_key, w_value, w_out, w_conv, t_query, t_key, t_value, t_out
):
    _, pixels, width = frames.shape
    scale = LOG2E / math.sqrt(width // HEADS)
    ndev = lax.axis_size("frame")
    weights = (w_conv, t_query, t_key, t_value, t_out)
    all_rows = gather_rows(ref_rows)
    query, kt, values, near_key, near_value = qkv(frames, w_query, w_key, w_value, scale)
    own = attend_own(query, kt, values)
    pieces = [a for rows in all_rows for a in ref_kv(rows, near_key, near_value)]
    first = attend_ref(frames, query, own, pieces, w_out)
    shared = exchange(first.reshape(ndev, pixels // ndev, width))
    done = temporal(shared, weights, scale)
    return exchange(done).reshape(1, pixels, width)


def solution(mesh):
    return jax.shard_map(
        per_device,
        mesh=mesh,
        in_specs=(P(("video", "frame"), None, None), P(("video", "frame"), None)) + (P(),) * 9,
        out_specs=P(("video", "frame"), None, None),
        check_vma=False,
    )
```
